32 devices in a mesh: tower: 2 (over y), narrow: 4 (over z), wide: 4 (over x, core).
Axes of the slice: x: 2, y: 2, z: 4, core: 2. Of those that a mesh axis runs over, the one named last changes fastest.
Arguments:
- features: bfloat16 [4, 8, 256, 2048], P('narrow', ('tower', 'wide')), may hold values from -6 to 6
- w_in: bfloat16 [2048, 4096], P(None, 'narrow'), may hold values from -0.125 to 0.125
- b_in: float32 [4096], P('narrow'), may hold values from -0.5 to 0.5
- w_out: bfloat16 [4096, 256], P('narrow'), may hold values from -0.09375 to 0.09375
- user_emb: bfloat16 [8192, 256], P('narrow'), as said below
- item_ids: int32 [4, 8, 256], P('narrow', ('tower', 'wide')), may hold values from 0 to 8191
Outputs:
- row_loss: float32 [8192], P('narrow')
- item_grad: float32 [4, 8, 256, 256], P('narrow', ('tower', 'wide'))
The draws below stay inside these ranges and needn't reach their ends.
Inputs may be any that keep to these rules, and one draw needn't show every extreme that they name: `user_emb`: user embeddings.
All inputs are finite; a program needn't handle non-finite values.
Results may differ from the reference program's by a relative error of at most 0.024.
Values may be sent and summed in bfloat16 or wider, within the bound.
A program may use at most 64 MiB of HBM per device.

```python
import math
import jax
import jax.numpy as jnp
import numpy as np
from jax import lax

F = 2048
HID = 4096
E = 256
BATCH = 8192
GROUPS = 4
PANELS = 8
SHARE = 256


def draw_user_emb(key, part):
    base = jnp.clip(jax.random.normal(key, (BATCH, E), jnp.float32), -6.0, 6.0)
    return base.astype(jnp.bfloat16)


def set_ends(values, own_key, low, high):
    spot = [jax.random.randint(jax.random.fold_in(own_key, axis), (), 0, length) for axis, length in enumerate(values.shape)]
    widest = values.shape.index(max(values.shape))
    beside = spot[:widest] + [(spot[widest] + 1) % values.shape[widest]] + spot[widest + 1:]
    return values.at[tuple(spot)].set(low).at[tuple(beside)].set(high)


def steps_of(own_key, extent, pieces, low, largest):
    def one(axis_at, shards_of):
        heights = jax.random.uniform(jax.random.fold_in(jax.random.fold_in(own_key, 6), axis_at), (shards_of,), jnp.float32, low / len(pieces), largest / len(pieces))
        return jnp.repeat(jnp.exp(heights), extent[axis_at] // shards_of).reshape((-1,) + (1,) * (len(extent) - axis_at - 1))

    factor_of = one(*pieces[0])
    for cut in pieces[1:]:
        factor_of = factor_of * one(*cut)
    return factor_of


def rank_table(number_of, slope):
    weights = [(1 << 20) // math.isqrt(grade ** slope) + 1 for grade in range(1, number_of + 1)]
    width = 1 + sum(weights) // (1 << 30)
    return np.cumsum(np.array([max(1, weight // width) for weight in weights]))


def ranked(stream_key, dims, count, slope):
    table = rank_table(count, slope)
    lot = jax.random.randint(jax.random.fold_in(stream_key, 1), dims, 0, int(table[count - 1]))
    grade = jnp.searchsorted(jnp.asarray(table, jnp.int32), lot, side="right")
    return jax.random.permutation(jax.random.fold_in(stream_key, 2), count)[grade].astype(jnp.int32)


def normal_values(key, extent, width, most, shards=(), kind=jnp.bfloat16):
    entries = jax.random.normal(key, extent, jnp.float32) * width
    if len(shards) > 0:
        entries = steps_of(key, extent, shards, -0.22, 0.18) * entries
    return jnp.clip(entries, min=-most, max=most).astype(kind)


def setup_inputs(seed: int = 0) -> dict:
    streams_of = jax.random.split(jax.random.key(seed), 7)
    features = normal_values(streams_of[0], (GROUPS, PANELS, SHARE, F), 1.0, 6.0, ((0, 4), (1, 8)))
    w_in = normal_values(streams_of[1], (F, HID), F ** -0.5, 0.125, ((1, 4),))
    b_in = jnp.clip(jax.random.uniform(streams_of[2], (HID,), jnp.float32, -0.5, 0.5) * steps_of(streams_of[2], (HID,), ((0, 4),), -0.4, 0.0), -0.5, 0.5)
    w_out = normal_values(streams_of[3], (HID, E), HID ** -0.5, 0.09375, ((0, 4),))
    user_emb = draw_user_emb(jax.random.fold_in(streams_of[6], 71), 0)
    item_ids = set_ends(ranked(streams_of[5], (GROUPS, PANELS, SHARE), BATCH, 4), jax.random.fold_in(streams_of[5], 3), 0, BATCH - 1).astype(jnp.int32)
    return {"features": features, "w_in": w_in, "b_in": b_in, "w_out": w_out, "user_emb": user_emb, "item_ids": item_ids}


INV_TEMP = 4.0
EPS = 1e-06
NEG = -1e+30

def unit_rows(embed):
    return embed * lax.rsqrt(lax.optimization_barrier(jnp.sum(embed * embed, axis=1, keepdims=True)) + EPS)

def reference(features, w_in, b_in, w_out, user_emb, item_ids):
    rows_in = features.reshape(BATCH, F)
    ids = item_ids.reshape(BATCH).astype(jnp.int32)
    hidden = jax.nn.relu(jnp.dot(rows_in, w_in, preferred_element_type=jnp.float32) + b_in).astype(jnp.bfloat16)
    embed = jnp.dot(hidden, w_out, preferred_element_type=jnp.float32)
    item_vec = unit_rows(embed).astype(jnp.bfloat16)
    block = min(512, BATCH)
    count = BATCH // block
    users = user_emb.reshape(count, block, E)
    row_ids = ids.reshape(count, block)
    row_glob = jnp.arange(BATCH, dtype=jnp.int32).reshape(count, block)
    col_glob = jnp.arange(BATCH, dtype=jnp.int32)

    def step(total, blk):
        user, rid, rglob = blk
        scores = jnp.dot(user, item_vec.T, preferred_element_type=jnp.float32) * INV_TEMP
        diag = rglob[:, None] == col_glob[None, :]
        keep = (rid[:, None] != ids[None, :]) | diag
        top = lax.optimization_barrier(jnp.max(jnp.where(keep, scores, NEG), axis=1))
        mass = lax.optimization_barrier(jnp.sum(jnp.where(keep, jnp.exp(scores - top[:, None]), 0.0), axis=1))
        lse = top + jnp.log(mass)
        pos = lax.optimization_barrier(jnp.sum(jnp.where(diag, scores, 0.0), axis=1))
        coef = (jnp.where(keep, jnp.exp(scores - lse[:, None]), 0.0) - diag.astype(jnp.float32)).astype(jnp.bfloat16)
        total = total + INV_TEMP * jnp.dot(coef.T, user, preferred_element_type=jnp.float32)
        return (total, lse - pos)
    total, losses = lax.scan(step, jnp.zeros((BATCH, E), jnp.float32), (users, row_ids, row_glob))
    return (losses.reshape(BATCH), total.reshape(GROUPS, PANELS, SHARE, E))
```

```python
import jax
import jax.numpy as jnp
from jax import lax
from jax.experimental import pallas as pl
from jax.experimental.pallas import tpu as pltpu
from jax.sharding import PartitionSpec as P

INV_TEMP = 4.0
EPS = 1e-06
NEG = -1e30


def unit_rows(embed):
    return embed * lax.rsqrt(jnp.sum(embed * embed, axis=1, keepdims=True) + EPS)


def block_scores(user, rid, rglob, vectors, col_ids, col_glob):
    scores = (
        lax.dot_general(user, vectors, (((1,), (1,)), ((), ())), preferred_element_type=jnp.float32)
        * INV_TEMP
    )
    diag = rglob[:, None] == col_glob[None, :]
    keep = (rid[:, None] != col_ids[None, :]) | diag
    return (scores, diag, keep)


def block_scores_cols(vectors, col_ids, col_glob, user, rid, rglob):
    scores = (
        lax.dot_general(vectors, user, (((1,), (1,)), ((), ())), preferred_element_type=jnp.float32)
        * INV_TEMP
    )
    diag = col_glob[:, None] == rglob[None, :]
    keep = (col_ids[:, None] != rid[None, :]) | diag
    return (scores, diag, keep)


def local(features, w_in, b_in, w_out, user_emb, item_ids):
    share = features.shape[2]
    width = features.shape[3]
    embed_width = w_out.shape[1]
    users_dev = user_emb.shape[0]
    groups = lax.axis_size("narrow")
    panel = groups * share
    gathered, gathered_ids = (
        lax.all_gather(features, "narrow", axis=0, tiled=True),
        lax.all_gather(item_ids, "narrow", axis=0, tiled=True),
    )
    rows_in = gathered.reshape(panel, width)
    col_ids = gathered_ids.reshape(panel)
    hidden = jax.nn.relu(jnp.dot(rows_in, w_in, preferred_element_type=jnp.float32) + b_in).astype(
        jnp.bfloat16
    )
    partial_embed = jnp.dot(hidden, w_out, preferred_element_type=jnp.float32)
    item_vec = unit_rows(lax.psum(partial_embed, "narrow")).astype(jnp.bfloat16)
    row_ids = lax.all_gather(item_ids, ("tower", "wide"), axis=1, tiled=True).reshape(users_dev)
    narrow_index = lax.axis_index("narrow")
    panel_index = lax.axis_index(("tower", "wide"))
    row_glob = narrow_index * users_dev + jnp.arange(users_dev, dtype=jnp.int32)
    column = jnp.arange(panel, dtype=jnp.int32)
    col_glob = column // share * users_dev + panel_index * share + column % share
    block = min(512, users_dev)
    count = users_dev // block
    users = user_emb.reshape(count, block, embed_width)
    rid_blocks = row_ids.reshape(count, block)
    rglob_blocks = row_glob.reshape(count, block)

    def local_stats(blk):
        user, rid, rglob = blk
        scores, diag, keep = block_scores(user, rid, rglob, item_vec, col_ids, col_glob)
        masked = jnp.where(keep, scores, NEG)
        top = jnp.max(masked, axis=1)
        mass = jnp.sum(jnp.where(keep, jnp.exp(scores - top[:, None]), 0.0), axis=1)
        pos = jnp.sum(jnp.where(diag, scores, 0.0), axis=1)
        return (top, mass, pos, masked.T)

    def local_stats_only(blk):
        top, mass, pos, masked = local_stats(blk)
        return (top, mass, pos)

    top, mass, pos = lax.map(local_stats_only, (users, rid_blocks, rglob_blocks))
    top = top.reshape(users_dev)
    mass = mass.reshape(users_dev)
    pos = pos.reshape(users_dev)
    global_top = lax.pmax(top, ("tower", "wide"))
    total, global_pos = lax.psum((mass * jnp.exp(top - global_top), pos), ("tower", "wide"))
    lse = global_top + jnp.log(total)
    row_loss = lse - global_pos
    lse_blocks = lse.reshape(count, block)

    def add_block(acc, blk):
        user, rid, rglob, lse_blk = blk
        scores, diag, keep = block_scores_cols(item_vec, col_ids, col_glob, user, rid, rglob)
        coef = (
            jnp.where(keep, jnp.exp(scores - lse_blk[None, :]), 0.0) - diag.astype(jnp.float32)
        ).astype(jnp.bfloat16)
        term = jnp.dot(coef, user, preferred_element_type=jnp.float32)
        return (acc + term, None)

    acc, unused = lax.scan(
        add_block,
        jnp.zeros((share * lax.axis_size("narrow"), embed_width), jnp.float32),
        (users, rid_blocks, rglob_blocks, lse_blocks),
    )
    own_grad = lax.psum_scatter(INV_TEMP * acc, "narrow", scatter_dimension=0, tiled=True)
    return (row_loss, own_grad.reshape(1, 1, share, embed_width))


MESH = pl.DeviceIdType.MESH
LOW = -1e20
ROW_PARTS = 2
PARTS = ROW_PARTS + 2


def coords(k):
    return {"narrow": k // 8, "tower": (k // 4) % 2, "wide": k % 4}


def fused(
    feat_ref, w_in_ref, b_in_ref, w_out_ref, users_ref, ids_ref, ids_col_ref,
    loss_ref, grad_ref,
    xg, wg, wog, bg, ug, idg, acc, core_in, y_out, y_in, vec, held, stats, stats_in, fin, fin_in,
    local_sem, fy_send, fy_recv, fc_send, fc_recv, wz_send, wz_recv, wx_send, wx_recv,
    uz_send, uz_recv, ux_send, ux_recv, uy_send, uy_recv, uc_send, uc_recv,
    rs_sem, small_send, small_recv,
):
    z = lax.axis_index("narrow")
    t = lax.axis_index("tower")
    wide = lax.axis_index("wide")
    x, c = wide // 2, wide % 2
    p = t * 4 + wide
    me = z * 8 + p
    ox, oc, ot = 1 - x, 1 - c, 1 - t
    xdev = {"wide": ox * 2 + c}
    cdev = {"wide": x * 2 + oc}
    ydev = {"tower": ot}
    share = feat_ref.shape[0]
    rows = wg.shape[2] // ROW_PARTS

    def peer(i):
        return lax.rem(me + i, 32)

    barrier = pltpu.get_barrier_semaphore()

    @pl.loop(1, 32)
    def _(i):
        pl.semaphore_signal(barrier, inc=1, device_id=coords(peer(i)), device_id_type=MESH)

    local = []

    def bring(src, dst):
        copy = pltpu.make_async_copy(src, dst, local_sem.at[len(local)])
        copy.start()
        local.append(copy)

    for i in range(2):
        unit = t * 4 + i * 2 + c
        bring(w_in_ref.at[:, pl.ds(pl.multiple_of(unit * 128, 128), 128)], wg.at[z, i])
        bring(w_out_ref.at[unit], wog.at[z, i])
        bring(b_in_ref.at[unit], bg.at[z, i])
    bring(feat_ref, xg.at[c * 2 + t])
    bring(users_ref, ug.at[pl.ds(z * 8, 8)])
    bring(ids_ref, idg.at[me])

    pl.semaphore_wait(barrier, 31)

    def remote(src, dst, send, recv, dev):
        return pltpu.make_async_remote_copy(
            src_ref=src, dst_ref=dst, send_sem=send, recv_sem=recv, device_id=dev, device_id_type=MESH
        )

    sent = []

    def send(make):
        make().start()
        sent.append(make)

    own = c * 2 + t
    send(lambda: remote(feat_ref, xg.at[own], fy_send, fy_recv, ydev))
    send(lambda: remote(feat_ref, xg.at[own], fc_send.at[0], fc_recv.at[0], cdev))

    for copy in local[:6]:
        copy.wait()

    def part(b, i, ch):
        if ch < ROW_PARTS:
            return wg.at[b, i, pl.ds(ch * rows, rows)]
        return wog.at[b, i] if ch == ROW_PARTS else bg.at[b, i]

    def z_copy(b, ch, to):
        return remote(
            part(b, x, ch), part(b, x, ch), wz_send.at[to - z + 1, b, ch], wz_recv.at[b, ch], {"narrow": to}
        )

    def x_copy(b, i, ch):
        return remote(part(b, i, ch), part(b, i, ch), wx_send.at[b, ch], wx_recv.at[b, ch], xdev)

    zsends = []

    def z_send(make, cond, ):
        pl.when(cond)(lambda: make().start())
        zsends.append((make, cond))

    order = [PARTS - 2, PARTS - 1] + list(range(ROW_PARTS))
    for ch in order:
        for to, cond in ((z - 1, z > 0), (z + 1, z < 3)):
            z_send(lambda ch=ch, to=to: z_copy(z, ch, to), cond)

    blocks = [1 + z % 2, (2 + 3 * z) % 5, 3 * (1 - z // 2)]
    onward = [jnp.where(b > z, z - 1, z + 1) for b in blocks]
    goes = [(to >= 0) & (to <= 3) for to in onward]

    def ids_copy(k):
        return remote(idg.at[me], idg.at[me], small_send.at[0], small_recv.at[0], coords(k))

    for copy in local[6:]:
        copy.wait()

    @pl.loop(1, 32)
    def _(i):
        ids_copy(peer(i)).start()

    def forward(j, z_part=True, mid=None):
        b, to, go = blocks[j], onward[j], goes[j]
        for ch in order:
            make = lambda ch=ch: z_copy(b, ch, to)
            x_copy_make = lambda ch=ch: x_copy(b, x, ch)
            z_copy(b, ch, z).wait_recv()
            pl.when(go)(lambda: make().start())
            x_copy_make().start()

    def forward_done(j):
        b, to, go = blocks[j], onward[j], goes[j]
        for ch in order:
            pl.when(go)(lambda: z_copy(b, ch, to).wait_send())
            x_copy(b, x, ch).wait_send()

    def x_arrived(j):
        for ch in order:
            x_copy(blocks[j], ox, ch).wait_recv()

    def compute(b, first=False):
        @pl.loop(0, 4)
        def _(s):
            weights = jnp.concatenate([wg[b, 0], wg[b, 1]], axis=1)
            bias = jnp.concatenate([bg[b, 0], bg[b, 1]], axis=1)
            outer = jnp.concatenate([wog[b, 0], wog[b, 1]], axis=0)
            h = jnp.dot(xg[s], weights, preferred_element_type=jnp.float32) + bias
            h = jnp.maximum(h, 0.0).astype(jnp.bfloat16)
            e = jnp.dot(h, outer, preferred_element_type=jnp.float32)
            acc[s] = e if first else acc[s] + e

    forward(0)
    forward(1)

    def u_z(n, to):
        k = n * 8 + p
        return remote(ug.at[k], ug.at[k], uz_send.at[to - z + 1, n], uz_recv.at[n], {"narrow": to})

    def slot(i, j):
        return (t + i - 2 * t * i) * 4 + (x + j - 2 * x * j) * 2 + c

    def u_x(n, j):
        k = n * 8 + slot(0, j)
        return remote(ug.at[k], ug.at[k], ux_send.at[n], ux_recv.at[n], xdev)

    def u_y(n, i, j):
        k = n * 8 + slot(i, j)
        return remote(ug.at[k], ug.at[k], uy_send.at[n, j], uy_recv.at[n, j], ydev)

    def u_c(n, i, j, lane):
        k = n * 8 + slot(i, j) - c + lane
        return remote(ug.at[k], ug.at[k], uc_send.at[n, i, j], uc_recv.at[n, i, j], cdev)

    for to, cond in ((z - 1, z > 0), (z + 1, z < 3)):
        z_send(lambda to=to: u_z(z, to), cond)

    def u_forward(j):
        n, to, go = blocks[j], onward[j], goes[j]
        u_z(n, z).wait_recv()
        z_send(lambda: u_z(n, to), go)
        send(lambda: u_x(n, 0))
        send(lambda: u_y(n, 0, 0))
        send(lambda: u_c(n, 0, 0, c))

    def u_cross(j):
        n = blocks[j]
        u_x(n, 1).wait_recv()
        send(lambda: u_y(n, 0, 1))
        send(lambda: u_c(n, 0, 1, c))

    def u_over(j):
        n = blocks[j]
        for k in range(2):
            u_y(n, 1, k).wait_recv()
            send(lambda k=k: u_c(n, 1, k, c))

    def u_ready(j):
        n = blocks[j]
        for i in range(2):
            for k in range(2):
                u_c(n, i, k, oc).wait_recv()

    middle = (z > 0) & (z < 3)
    edge = (z == 0) | (z == 3)
    pl.when(middle)(lambda: forward(2))

    y_slot = c * 2 + ot
    remote(xg.at[y_slot], xg.at[y_slot], fy_send, fy_recv, ydev).wait_recv()
    send(lambda: remote(xg.at[y_slot], xg.at[y_slot], fc_send.at[1], fc_recv.at[1], cdev))
    for i, other in enumerate((oc * 2 + t, oc * 2 + ot)):
        remote(xg.at[other], xg.at[other], fc_send.at[i], fc_recv.at[i], cdev).wait_recv()

    compute(z, first=True)
    x_arrived(0)
    compute(blocks[0])
    x_arrived(1)
    compute(blocks[1])
    pl.when(edge)(lambda: forward(2))
    u_forward(0)
    x_arrived(2)
    compute(blocks[2])

    core_copy = lambda: remote(acc.at[pl.ds(oc * 2, 2)], core_in, rs_sem.at[0], rs_sem.at[1], cdev)
    send(core_copy)
    u_forward(1)
    u_cross(0)
    core_copy().wait_recv()
    y_out[...] = acc[c * 2 + ot] + core_in[ot]
    y_copy = lambda: remote(y_out, y_in, rs_sem.at[2], rs_sem.at[3], ydev)
    send(y_copy)
    u_forward(2)
    u_cross(1)
    u_over(0)
    y_copy().wait_recv()
    embed = acc[own] + core_in[t] + y_in[...]
    norm = lax.rsqrt(jnp.sum(embed * embed, axis=1, keepdims=True) + EPS)
    vec[...] = (embed * norm).astype(jnp.bfloat16)

    def ids_all():
        ref = idg.at[pl.ds(0, 31)]
        return pltpu.make_async_copy(ref, ref, small_recv.at[0])

    ids_all().wait()
    spread = lax.broadcasted_iota(jnp.int32, (share, share), 0) - lax.broadcasted_iota(
        jnp.int32, (share, share), 1
    )

    def raw(k):
        s = lax.dot_general(vec[...], ug[k], (((1,), (1,)), ((), ())), preferred_element_type=jnp.float32)
        return s * INV_TEMP

    def score(k):
        s = raw(k)
        keep = (ids_col_ref[...] != idg[k]) | (spread == (k - me) * 512)
        s = jnp.where(keep, s, NEG)
        top = jnp.maximum(jnp.max(s, axis=0, keepdims=True), LOW)
        e = jnp.exp(s - top)
        held[k] = e
        stats[k, 0:1] = top
        stats[k, 1:2] = jnp.sum(e, axis=0, keepdims=True)

    def score_block(n):
        @pl.loop(0, 4)
        def _(i):
            for half in range(2):
                score(n * 8 + i * 2 + half)

    score_block(z)
    fin[1:2] = jnp.sum(jnp.where(spread == 0, raw(me), 0.0), axis=0, keepdims=True)
    u_cross(2)
    u_over(1)
    u_over(2)
    for j in range(3):
        u_ready(j)
        score_block(blocks[j])

    def stats_copy(k):
        return remote(stats.at[k], stats_in.at[me], small_send.at[1], small_recv.at[1], coords(k))

    @pl.loop(1, 32)
    def _(i):
        stats_copy(peer(i)).start()

    stats_in[me] = stats[me]
    ref_in = stats_in.at[pl.ds(0, 31)]
    pltpu.make_async_copy(ref_in, ref_in, small_recv.at[1]).wait()
    got = stats_in[...]
    tops, sums = got[:, 0, :], got[:, 1, :]
    top = jnp.max(tops, axis=0, keepdims=True)
    total = jnp.sum(sums * jnp.exp(tops - top), axis=0, keepdims=True)
    lse = top + jnp.log(total)
    fin[0:1] = lse
    fin[1:2] = lse - fin[1:2]
    fin_in[me] = fin[...]

    def fin_copy(k):
        return remote(fin, fin_in.at[me], small_send.at[2], small_recv.at[2], coords(k))

    @pl.loop(1, 32)
    def _(i):
        fin_copy(peer(i)).start()

    ref_fin = fin_in.at[pl.ds(0, 31)]
    pltpu.make_async_copy(ref_fin, ref_fin, small_recv.at[2]).wait()

    grad_ref[...] = -ug[me].astype(jnp.float32)

    @pl.loop(0, 8)
    def _(i):
        coefs, users = [], []
        for q in range(4):
            k = i * 4 + q
            factor = jnp.exp(stats[k, 0:1] - fin_in[k, 0:1])
            coefs.append((held[k] * factor).astype(jnp.bfloat16))
            users.append(ug[k])
        grad_ref[...] += jnp.dot(
            jnp.concatenate(coefs, axis=1), jnp.concatenate(users, axis=0), preferred_element_type=jnp.float32
        )

    grad_ref[...] = grad_ref[...] * INV_TEMP
    loss_ref[...] = fin_in[pl.ds(z * 8, 8), 1, :]

    for make in sent:
        make().wait_send()
    for make, cond in zsends:
        pl.when(cond)(lambda make=make: make().wait_send())
    for j in range(3):
        forward_done(j)
    for buf, sem in ((idg, 0), (stats_in, 1), (fin_in, 2)):
        ref = buf.at[pl.ds(0, 31)]
        pltpu.make_async_copy(ref, ref, small_send.at[sem]).wait()


def local_fused(features, w_in, b_in, w_out, user_emb, item_ids):
    share, width = features.shape[2:]
    embed = w_out.shape[1]
    f32, bf16, i32 = jnp.float32, jnp.bfloat16, jnp.int32
    hbm = pl.BlockSpec(memory_space=pl.ANY)
    vmem = pl.BlockSpec(memory_space=pltpu.VMEM)
    dma = pltpu.SemaphoreType.DMA
    row_loss, grad = pl.pallas_call(
        fused,
        out_shape=(
            jax.ShapeDtypeStruct((8, share), f32),
            jax.ShapeDtypeStruct((share, embed), f32),
        ),
        in_specs=[hbm, hbm, hbm, hbm, hbm, hbm, vmem],
        out_specs=(vmem, vmem),
        scratch_shapes=[
            pltpu.VMEM((4, share, width), bf16),
            pltpu.VMEM((4, 2, width, 128), bf16),
            pltpu.VMEM((4, 2, 128, embed), bf16),
            pltpu.VMEM((4, 2, 1, 128), f32),
            pltpu.VMEM((32, share, embed), bf16),
            pltpu.VMEM((32, 1, share), i32),
            pltpu.VMEM((4, share, embed), f32),
            pltpu.VMEM((2, share, embed), f32),
            pltpu.VMEM((share, embed), f32),
            pltpu.VMEM((share, embed), f32),
            pltpu.VMEM((share, embed), bf16),
            pltpu.VMEM((32, share, share), f32),
            pltpu.VMEM((32, 2, share), f32),
            pltpu.VMEM((32, 2, share), f32),
            pltpu.VMEM((2, share), f32),
            pltpu.VMEM((32, 2, share), f32),
            dma((9,)),
            dma, dma, dma((2,)), dma((2,)),
            dma((3, 4, PARTS)), dma((4, PARTS)), dma((4, PARTS)), dma((4, PARTS)),
            dma((3, 4)), dma((4,)), dma((4,)), dma((4,)),
            dma((4, 2)), dma((4, 2)), dma((4, 2, 2)), dma((4, 2, 2)),
            dma((4,)), dma((3,)), dma((3,)),
        ],
        compiler_params=pltpu.CompilerParams(
            collective_id=0, has_side_effects=True, vmem_limit_bytes=44 * 1024 * 1024
        ),
        cost_estimate=pl.CostEstimate(flops=8 * 10**9, bytes_accessed=4 * 10**6, transcendentals=2 * 10**6),
    )(
        features.reshape(share, width),
        w_in,
        b_in.reshape(8, 1, 128),
        w_out.reshape(8, 128, embed),
        user_emb.reshape(8, share, embed),
        item_ids.reshape(1, share),
        item_ids.reshape(share, 1),
    )
    return row_loss.reshape(8 * share), grad.reshape(1, 1, share, embed)


def fits(mesh):
    return dict(mesh.shape) == {"tower": 2, "narrow": 4, "wide": 4}


def solution(mesh):
    return jax.shard_map(
        local_fused if fits(mesh) else local,
        mesh=mesh,
        in_specs=(
            P("narrow", ("tower", "wide"), None, None),
            P(None, "narrow"),
            P("narrow"),
            P("narrow", None),
            P("narrow", None),
            P("narrow", ("tower", "wide"), None),
        ),
        out_specs=(P("narrow"), P("narrow", ("tower", "wide"), None, None)),
        check_vma=False,
    )
```
